1024 devices in a mesh: dp: 32 (over x, y, core), fsdp: 32 (over z).
Axes of the slice: x: 4, y: 4, z: 32, core: 2. Of those that a mesh axis runs over, the one named last changes fastest.
Arguments:
- events: bfloat16 [3072, 128, 1024], P(('dp', 'fsdp')), may hold values from -6 to 6
- query_weight: bfloat16 [1024, 512], P('fsdp'), may hold values from -0.1875 to 0.1875
- keys: bfloat16 [3072, 128, 512], P(('dp', 'fsdp')), may hold values from -6 to 6
- values: bfloat16 [3072, 128, 512], P(('dp', 'fsdp')), may hold values from -48 to 48
- gates: bfloat16 [3072, 128, 512], P(('dp', 'fsdp')), may hold values from -6 to 6
- cotangent: bfloat16 [3072, 128, 512], P(('dp', 'fsdp')), may hold values from -6 to 6
- lengths: int32 [3072], replicated, may hold values from 1 to 128, as said below
Outputs:
- grad_keys: bfloat16 [3072, 128, 512], P(('dp', 'fsdp'))
- grad_values: bfloat16 [3072, 128, 512], P(('dp', 'fsdp'))
- grad_gates: bfloat16 [3072, 128, 512], P(('dp', 'fsdp'))
- grad_weight: float32 [1024, 512], P('fsdp')
The draws below stay inside these ranges and needn't reach their ends.
Inputs may be any that keep to these rules, and one draw needn't show every extreme that they name: Each sequence fills the first lengths[b] events of its slot of 128 events; the rest is padding that no output reads.
All inputs are finite; a program needn't handle non-finite values.
Results may differ from the reference program's by a relative error of at most 0.015.
Values may be sent and summed in bfloat16 or wider, within the bound.
A program may use at most 32 MiB of HBM per device.

```python
import math
import jax
import jax.numpy as jnp
from jax import lax

D = 1024
HEADS = 4
HEAD_DIM = 128
BLK = 64
MAXB = 2
SLOTS = 3
SPAN = 128
HW = 512
SEQS = 3072


def draw_lengths(key, part):
    key = jax.random.fold_in(key, 7)
    split_keys = jax.random.split(key, 5)
    device_total = SEQS // SLOTS
    loaded = jax.random.randint(split_keys[0], (device_total, 1), 0, 4) == 0
    long_lengths = jax.random.randint(split_keys[1], (device_total, SLOTS), BLK + 1, MAXB * BLK + 1)
    short_lengths = jax.random.randint(split_keys[2], (device_total, SLOTS), 1, BLK + 1)
    drawn = jnp.where(loaded, long_lengths, short_lengths).reshape(SEQS)
    longest_at = jax.random.randint(split_keys[3], (), 0, SEQS // 2)
    shortest_at = SEQS // 2 + jax.random.randint(split_keys[4], (), 0, SEQS // 2)
    drawn = drawn.at[longest_at].set(MAXB * BLK).at[shortest_at].set(1)
    return drawn.astype(jnp.int32)


def shard_levels(rng, extent, pieces, low, largest):
    def one(dim, parts):
        draws = jax.random.uniform(jax.random.fold_in(jax.random.fold_in(rng, 6), dim), (parts,), jnp.float32, low / len(pieces), largest / len(pieces))
        return jnp.repeat(jnp.exp(draws), extent[dim] // parts).reshape((-1,) + (1,) * (len(extent) - dim - 1))

    gain = one(*pieces[0])
    for cut in pieces[1:]:
        gain = gain * one(*cut)
    return gain


def normal_values(own_key, dims, scale, reach, cuts=(), held_as=jnp.bfloat16):
    entries = jax.random.normal(own_key, dims, jnp.float32) * scale
    if len(cuts) > 0:
        entries = shard_levels(own_key, dims, cuts, -0.22, 0.18) * entries
    return jnp.clip(entries, min=-reach, max=reach).astype(held_as)


def setup_inputs(seed: int = 0) -> dict:
    key_of = jax.random.split(jax.random.key(seed), 8)
    events = normal_values(key_of[0], (SEQS, SPAN, D), 1.0, 6.0, ((0, 1024),))
    query_weight = normal_values(key_of[1], (D, HW), D ** -0.5, 0.1875, ((0, 32),))
    keys = normal_values(key_of[2], (SEQS, SPAN, HW), 1.0, 6.0, ((0, 1024),))
    values = normal_values(key_of[3], (SEQS, SPAN, HW), 8.0, 48.0, ((0, 1024),))
    gates = normal_values(key_of[4], (SEQS, SPAN, HW), 1.0, 6.0, ((0, 1024),))
    cotangent = normal_values(key_of[5], (SEQS, SPAN, HW), 1.0, 6.0, ((0, 1024),))
    lengths = draw_lengths(jax.random.fold_in(key_of[7], 71), 0)
    return dict(events=events, query_weight=query_weight, keys=keys, values=values, gates=gates, cotangent=cotangent, lengths=lengths)


EPSILON = 1e-06

def rounded(values_in):
    return lax.optimization_barrier(values_in.astype(jnp.bfloat16)).astype(jnp.float32)

def slot_grads(queries, key_rows, value_rows, gate_rows, upstream_rows, length, head_count):
    row_count = queries.shape[0]
    head_width = queries.shape[1]
    head_depth = head_width // head_count
    score_scale = 1.0 / math.sqrt(head_depth)
    query_h = queries.astype(jnp.float32).reshape(row_count, head_count, head_depth)
    keys_h = key_rows.astype(jnp.float32).reshape(row_count, head_count, head_depth)
    values_h = value_rows.astype(jnp.float32).reshape(row_count, head_count, head_depth)
    scores = jnp.einsum('qhd,khd->hqk', query_h, keys_h) * score_scale
    places = lax.iota(jnp.int32, row_count)
    causal = (places[None, :] <= places[:, None]) & (places[:, None] < length)
    weight_mask = causal.astype(jnp.float32)[None]
    inverse = 1.0 / length.astype(jnp.float32)
    sigmoid = jax.nn.sigmoid(scores)
    attention = rounded(scores * sigmoid * weight_mask * inverse)
    mixed_rows = jnp.einsum('hqk,khd->qhd', attention, values_h).reshape(row_count, head_width)
    centred = mixed_rows - lax.optimization_barrier(jnp.mean(mixed_rows, axis=1, keepdims=True))
    inv_std = lax.rsqrt(lax.optimization_barrier(jnp.mean(centred * centred, axis=1, keepdims=True)) + EPSILON)
    normed = centred * inv_std
    upstream = upstream_rows.astype(jnp.float32)
    grad_gates = (upstream * normed).astype(jnp.bfloat16)
    valid_rows = (places < length).astype(jnp.float32)[:, None]
    grad_normed = upstream * gate_rows.astype(jnp.float32) * valid_rows
    grad_mixed = inv_std * (grad_normed - lax.optimization_barrier(jnp.mean(grad_normed, axis=1, keepdims=True)) - normed * lax.optimization_barrier(jnp.mean(grad_normed * normed, axis=1, keepdims=True)))
    grad_mixed = rounded(grad_mixed).reshape(row_count, head_count, head_depth)
    grad_values = jnp.einsum('hqk,qhd->khd', attention, grad_mixed)
    grad_attention = jnp.einsum('qhd,khd->hqk', grad_mixed, values_h)
    grad_scores = rounded(grad_attention * sigmoid * (1.0 + scores * (1.0 - sigmoid)) * weight_mask * inverse)
    grad_query = jnp.einsum('hqk,khd->qhd', grad_scores, keys_h) * score_scale
    grad_keys = jnp.einsum('hqk,qhd->khd', grad_scores, query_h) * score_scale
    return (grad_query.reshape(row_count, head_width).astype(jnp.bfloat16), grad_keys.reshape(row_count, head_width).astype(jnp.bfloat16), grad_values.reshape(row_count, head_width).astype(jnp.bfloat16), grad_gates)

def reference(events, query_weight, keys, values, gates, cotangent, lengths):

    def one_sequence(running, operands):
        tokens, key_rows, value_rows, gate_rows, upstream_rows, length = operands
        queries = lax.optimization_barrier(jnp.dot(tokens, query_weight, preferred_element_type=jnp.float32).astype(jnp.bfloat16))
        grad_query, grad_keys, grad_values, grad_gates = slot_grads(queries, key_rows, value_rows, gate_rows, upstream_rows, length, HEADS)
        running = running + jnp.dot(tokens.T, grad_query, preferred_element_type=jnp.float32)
        return (running, (grad_keys, grad_values, grad_gates))
    initial = jnp.zeros((D, HEADS * HEAD_DIM), jnp.float32)
    running, outputs = lax.scan(one_sequence, initial, (events, keys, values, gates, cotangent, lengths))
    return (outputs[0], outputs[1], outputs[2], running / SEQS)
```

```python
import functools
import math

import jax
import jax.numpy as jnp
from jax import lax
from jax.experimental import pallas as pl
from jax.experimental.pallas import tpu as pltpu
from jax.sharding import PartitionSpec as P

MESH = pl.DeviceIdType.MESH
HEADS = 4
DEPTH = 128
SLOTS = 3
SPAN = 128
ROWS = SLOTS * SPAN
WIDTH = HEADS * DEPTH
MODEL = 1024
CHIPS = 16
PLANE = 32
RING = 32
EPSILON = 1e-06
SCALE = 1.0 / math.sqrt(DEPTH)
F32 = jnp.float32
BF16 = jnp.bfloat16


def dot(a, b, ca, cb):
    return lax.dot_general(a, b, (((ca,), (cb,)), ((), ())), preferred_element_type=F32)


def layer_kernel(
    total_seqs,
    events_hbm, weight_hbm, keys_hbm, values_hbm, gates_hbm, upstream_hbm, lengths_hbm,
    grad_keys_hbm, grad_values_hbm, grad_gates_hbm, grad_weight_ref,
    ev, kk, vv, gg, uu, lens,
    wf, wun, evt, gn, qq, att, dact, gm, gs, gq, out_k, out_v, out_g,
    gbuf, cbuf, sbuf, rbuf, tbuf, zbuf, gw,
    in_sem, near_s, near_r, rel_s, rel_r, agn_s, agn_r, agf_s, agf_r, cw_s, cw_r,
    cg_s, cg_r, rs_s, rs_r, zr_s, zr_r, fin_s, fin_r, out_sem,
):
    dp = lax.axis_index("dp")
    z = lax.axis_index("fsdp")
    core = lax.rem(dp, 2)
    chip = dp // 2
    x = chip // 4
    y = lax.rem(chip, 4)
    phase = lax.rem(y - z + RING, 4)
    is_source = lax.rem(z, 4) == y

    def ring_at(offset):
        return {"dp": dp, "fsdp": lax.rem(z + offset + RING, RING)}

    def chip_at(other, other_core):
        return {"dp": other * 2 + other_core, "fsdp": z}

    def remote(src, dst, ssem, rsem, device):
        return pltpu.make_async_remote_copy(
            src_ref=src, dst_ref=dst, send_sem=ssem, recv_sem=rsem,
            device_id=device, device_id_type=MESH,
        )

    partner = chip_at(chip, 1 - core)

    loads = [
        pltpu.make_async_copy(src, dst, in_sem.at[i])
        for i, (src, dst) in enumerate(
            (
                (lengths_hbm, lens), (gates_hbm, gg), (upstream_hbm, uu),
                (events_hbm, ev), (keys_hbm, kk), (values_hbm, vv),
            )
        )
    ]
    for load in loads:
        load.start()

    barrier = pltpu.get_barrier_semaphore()

    def tell(device):
        pl.semaphore_signal(barrier, inc=1, device_id=device, device_id_type=MESH)

    for j in (-2, -1, 1):
        tell(ring_at(phase + 4 * j))

    @pl.when(phase != 0)
    def _():
        tell(ring_at(phase))

    tell(ring_at(8))
    tell(ring_at(-8))
    for i in range(1, CHIPS):
        tell(chip_at(lax.rem(chip + i, CHIPS), core))
    tell(partner)
    pl.semaphore_wait(barrier, jnp.where(is_source, 33, 18))

    tile = weight_hbm.at[pl.ds(pl.multiple_of(core * 16, 16), 16), pl.ds(pl.multiple_of(x * 128, 128), 128)]
    own_tile = pltpu.make_async_copy(tile, wf.at[2, 0, core, x], near_r.at[2])
    near_sends = []
    for e in range(-7, 9):
        if e != 0:
            t = 8 - e
            near_sends.append(
                remote(tile, wf.at[t // 4, t % 4, core, x], near_s.at[t], near_r.at[t // 4], ring_at(e))
            )

    @pl.when(is_source)
    def _():
        for send in near_sends:
            send.start()
        own_tile.start()

    row_ids = lax.broadcasted_iota(jnp.int32, (SPAN, DEPTH), 0)
    col_ids = lax.broadcasted_iota(jnp.int32, (SPAN, DEPTH), 1)
    loads[0].wait()
    loads[1].wait()
    loads[2].wait()
    first_seq = (dp * RING + z) * SLOTS
    own_lens = [lens[first_seq + b] for b in range(SLOTS)]
    for b in range(SLOTS):
        rows = pl.ds(b * SPAN, SPAN)
        valid = row_ids < own_lens[b]
        parts = []
        for h in range(HEADS):
            cols = pl.ds(h * DEPTH, DEPTH)
            product = uu[rows, cols].astype(F32) * gg[rows, cols].astype(F32)
            parts.append(jnp.where(valid, product, 0.0))
        mean = jnp.sum(parts[0] + parts[1] + parts[2] + parts[3], axis=1, keepdims=True) * (1.0 / WIDTH)
        for h in range(HEADS):
            gn[rows, pl.ds(h * DEPTH, DEPTH)] = parts[h] - mean

    def near_arrived(jj):
        here = wf.at[jj, phase, core, x]
        remote(here, here, near_s.at[0], near_r.at[jj], partner).wait_recv()

    near_arrived(2)
    near_arrived(3)
    relay_down = remote(
        wf.at[pl.ds(2, 2), phase, core, x], wf.at[pl.ds(4, 2), phase, core, x], rel_s.at[0], rel_r.at[0], ring_at(-8)
    )
    relay_down.start()
    near_arrived(0)
    near_arrived(1)
    relay_up = remote(
        wf.at[pl.ds(0, 2), phase, core, x], wf.at[pl.ds(6, 2), phase, core, x], rel_s.at[1], rel_r.at[1], ring_at(8)
    )
    relay_up.start()

    def spread(first, ssem, rsem):
        piece = wf.at[pl.ds(first, 4), phase, core, x]
        sends = [
            remote(piece, piece, ssem.at[i], rsem.at[i], chip_at(lax.rem(chip + i, CHIPS), core))
            for i in range(1, CHIPS)
        ]
        for send in sends:
            send.start()
        return sends

    def gathered(first, ssem, rsem):
        for i in range(1, CHIPS):
            other = lax.rem(chip - i + CHIPS, CHIPS)
            there = wf.at[pl.ds(first, 4), lax.rem(lax.rem(other, 4) - z + RING, 4), core, other // 4]
            remote(there, there, ssem.at[i], rsem.at[i], partner).wait_recv()

    near_spread = spread(0, agn_s, agn_r)
    loads[3].wait()
    for m in range(0, MODEL, 128):
        evt[pl.ds(m, 128), :] = ev[:, pl.ds(m, 128)].T
    relay_down.wait_recv()
    relay_up.wait_recv()
    far_spread = spread(4, agf_s, agf_r)
    gathered(0, agn_s, agn_r)
    swaps = []

    def swap(first, index):
        mine = wf.at[pl.ds(first, 4), :, core]
        copy = remote(mine, mine, cw_s.at[index], cw_r.at[index], partner)
        copy.start()
        swaps.append(copy)

    swap(0, 0)
    gathered(4, agf_s, agf_r)
    swap(4, 1)
    loads[4].wait()
    loads[5].wait()
    swaps[0].wait_recv()
    swaps[1].wait_recv()

    for shard in range(RING):
        t = lax.rem(shard - z + 8 + RING, RING)
        for half in range(2):
            for c in range(4):
                wun[pl.ds(shard * 32 + half * 16, 16), pl.ds(c * 128, 128)] = wf[t // 4, lax.rem(t, 4), half, c]

    qq[...] = dot(ev[...], wun[...], 1, 0).astype(BF16)
    for b in range(SLOTS):
        rows = pl.ds(b * SPAN, SPAN)
        inverse = 1.0 / jnp.full((1, DEPTH), own_lens[b].astype(F32))
        weight = jnp.where((col_ids <= row_ids) & (row_ids < own_lens[b]), inverse, 0.0)
        mixed = []
        for h in range(HEADS):
            cols = pl.ds(h * DEPTH, DEPTH)
            scores = dot(qq[rows, cols], kk[rows, cols], 1, 1) * SCALE
            sigmoid = 0.5 * jnp.tanh(0.5 * scores) + 0.5
            weighted = sigmoid * weight
            attention = (scores * weighted).astype(BF16)
            att[b * HEADS + h] = attention
            dact[b * HEADS + h] = weighted * (1.0 + scores * (1.0 - sigmoid))
            mixed.append(dot(attention, vv[rows, cols], 1, 0))
        mean = jnp.sum(mixed[0] + mixed[1] + mixed[2] + mixed[3], axis=1, keepdims=True) * (1.0 / WIDTH)
        centred = [m - mean for m in mixed]
        squares = [m * m for m in centred]
        var = jnp.sum(squares[0] + squares[1] + squares[2] + squares[3], axis=1, keepdims=True) * (1.0 / WIDTH)
        inv_std = lax.rsqrt(var + EPSILON)
        normed = [m * inv_std for m in centred]
        grads = [gn[rows, pl.ds(h * DEPTH, DEPTH)] for h in range(HEADS)]
        overlap = [g * n for g, n in zip(grads, normed)]
        slope = jnp.sum(overlap[0] + overlap[1] + overlap[2] + overlap[3], axis=1, keepdims=True) * (1.0 / WIDTH)
        for h in range(HEADS):
            cols = pl.ds(h * DEPTH, DEPTH)
            gm[rows, cols] = (inv_std * (grads[h] - normed[h] * slope)).astype(BF16)
            out_g[rows, cols] = (uu[rows, cols].astype(F32) * normed[h]).astype(BF16)

    core_sends = []
    rs_sends = []

    def reduce_head(h):
        core_sends[h].wait_recv()
        summed = gbuf[h, :, :, core].astype(F32) + cbuf[h].astype(F32)
        sbuf[h] = summed.astype(BF16)
        for r in range(4):
            target = ((h - r) % 4) * 4 + r
            send = remote(
                sbuf.at[h, :, r], rbuf.at[chip], rs_s.at[h * 4 + r], rs_r.at[chip], chip_at(target, core)
            )
            rs_sends.append((target, send))

            @pl.when(chip != target)
            def _():
                send.start()

    for h in range(HEADS):
        cols = pl.ds(h * DEPTH, DEPTH)
        for b in range(SLOTS):
            rows = pl.ds(b * SPAN, SPAN)
            grad_attention = dot(gm[rows, cols], vv[rows, cols], 1, 1)
            grad_scores = (grad_attention * dact[b * HEADS + h]).astype(BF16)
            gs[b * HEADS + h] = grad_scores
            gq[rows, :] = (dot(grad_scores, kk[rows, cols], 1, 0) * SCALE).astype(BF16)
        gbuf[h] = dot(evt[...], gq[...], 1, 0).astype(BF16).reshape(8, 4, 2, 16, 128)
        send = remote(gbuf.at[h, :, :, 1 - core], cbuf.at[h], cg_s.at[h], cg_r.at[h], partner)
        send.start()
        core_sends.append(send)
        if h > 0:
            reduce_head(h - 1)
    reduce_head(HEADS - 1)

    head = lax.rem(x + y, 4)
    total = sbuf[head, :, y].astype(F32)
    for i in range(1, CHIPS):
        other = lax.rem(chip + i, CHIPS)
        there = rbuf.at[other]
        remote(there, there, rs_s.at[0], rs_r.at[other], partner).wait_recv()
        total = total + rbuf[other].astype(F32)
    tbuf[...] = total.astype(BF16)
    ring_sends = []
    for k in range(8):
        target = 4 * k + y
        send = remote(tbuf.at[k], zbuf.at[z], zr_s.at[k], zr_r.at[z], {"dp": dp, "fsdp": target})
        ring_sends.append((target, send))

        @pl.when(target != z)
        def _():
            send.start()

    for b in range(SLOTS):
        rows = pl.ds(b * SPAN, SPAN)
        for h in range(HEADS):
            cols = pl.ds(h * DEPTH, DEPTH)
            out_v[rows, cols] = dot(att[b * HEADS + h], gm[rows, cols], 0, 0).astype(BF16)
            out_k[rows, cols] = (dot(gs[b * HEADS + h], qq[rows, cols], 0, 0) * SCALE).astype(BF16)
    stores = [
        pltpu.make_async_copy(src, dst, out_sem.at[i])
        for i, (src, dst) in enumerate(((out_k, grad_keys_hbm), (out_v, grad_values_hbm), (out_g, grad_gates_hbm)))
    ]
    for store in stores:
        store.start()

    final_sends = []
    for i in range(1, PLANE):
        there = gw.at[core, head]
        final_sends.append(
            remote(there, there, fin_s.at[i], fin_r.at[x * 2 + core], {"dp": lax.rem(dp + i, PLANE), "fsdp": z})
        )

    @pl.when(is_source)
    def _():
        acc = tbuf[z // 4].astype(F32)
        for i in range(1, RING):
            other = lax.rem(z + i, RING)
            there = zbuf.at[other]
            remote(there, there, zr_s.at[0], zr_r.at[other], partner).wait_recv()
            acc = acc + zbuf[other].astype(F32)
        gw[core, head] = acc * (1.0 / total_seqs)
        for send in final_sends:
            send.start()

    source_y = lax.rem(z, 4)
    for sx in range(4):
        for sc in range(2):
            @pl.when((chip != sx * 4 + source_y) | (core != sc))
            def _():
                there = gw.at[sc, lax.rem(sx + source_y, 4)]
                remote(there, there, fin_s.at[0], fin_r.at[sx * 2 + sc], partner).wait_recv()
    for half in range(2):
        for h in range(HEADS):
            grad_weight_ref[pl.ds(half * 16, 16), pl.ds(h * DEPTH, DEPTH)] = gw[half, h]

    @pl.when(is_source)
    def _():
        for send in near_sends:
            send.wait_send()
        for send in final_sends:
            send.wait_send()

    relay_down.wait_send()
    relay_up.wait_send()
    for send in near_spread + far_spread + swaps + core_sends:
        send.wait_send()
    for target, send in rs_sends:
        @pl.when(chip != target)
        def _():
            send.wait_send()
    for target, send in ring_sends:
        @pl.when(target != z)
        def _():
            send.wait_send()
    for store in stores:
        store.wait()


def shards(events, query_weight, keys, values, gates, cotangent, lengths):
    flat = [a.reshape(ROWS, a.shape[2]) for a in (events, keys, values, gates, cotangent)]
    hbm = pl.BlockSpec(memory_space=pl.ANY)
    vmem = pltpu.VMEM
    dma = pltpu.SemaphoreType.DMA
    row_out = jax.ShapeDtypeStruct((ROWS, WIDTH), BF16)
    scratch = [
        vmem((ROWS, MODEL), BF16), vmem((ROWS, WIDTH), BF16), vmem((ROWS, WIDTH), BF16),
        vmem((ROWS, WIDTH), BF16), vmem((ROWS, WIDTH), BF16), pltpu.SMEM(lengths.shape, jnp.int32),
        vmem((8, 4, 2, 4, 16, 128), BF16), vmem((MODEL, WIDTH), BF16), vmem((MODEL, ROWS), BF16),
        vmem((ROWS, WIDTH), F32), vmem((ROWS, WIDTH), BF16), vmem((12, SPAN, SPAN), BF16),
        vmem((12, SPAN, SPAN), F32), vmem((ROWS, WIDTH), BF16), vmem((12, SPAN, SPAN), BF16),
        vmem((ROWS, DEPTH), BF16),
        vmem((ROWS, WIDTH), BF16), vmem((ROWS, WIDTH), BF16), vmem((ROWS, WIDTH), BF16),
        vmem((4, 8, 4, 2, 16, 128), BF16), vmem((4, 8, 4, 16, 128), BF16), vmem((4, 8, 4, 16, 128), BF16),
        vmem((16, 8, 16, 128), BF16), vmem((8, 16, 128), BF16), vmem((RING, 16, 128), BF16),
        vmem((2, 4, 16, 128), F32),
        dma((6,)), dma((16,)), dma((4,)), dma((2,)), dma((2,)), dma((16,)), dma((16,)), dma((16,)), dma((16,)),
        dma((2,)), dma((2,)), dma((4,)), dma((4,)), dma((16,)), dma((16,)), dma((8,)), dma((32,)),
        dma((32,)), dma((8,)), dma((3,)),
    ]
    grad_keys, grad_values, grad_gates, grad_weight = pl.pallas_call(
        functools.partial(layer_kernel, lengths.shape[0]),
        out_shape=(row_out, row_out, row_out, jax.ShapeDtypeStruct((32, WIDTH), F32)),
        in_specs=[hbm] * 7,
        out_specs=(hbm, hbm, hbm, pl.BlockSpec(memory_space=vmem)),
        scratch_shapes=scratch,
        compiler_params=pltpu.CompilerParams(
            collective_id=0, has_side_effects=True, vmem_limit_bytes=48 * 2**20
        ),
        name="layer",
    )(flat[0], query_weight, flat[1], flat[2], flat[3], flat[4], lengths)
    shape = keys.shape
    return grad_keys.reshape(shape), grad_values.reshape(shape), grad_gates.reshape(shape), grad_weight


def solution(mesh):
    by_seq = P(("dp", "fsdp"), None, None)
    return jax.shard_map(
        shards,
        mesh=mesh,
        in_specs=(by_seq, P("fsdp", None), by_seq, by_seq, by_seq, by_seq, P()),
        out_specs=(by_seq, by_seq, by_seq, P("fsdp", None)),
        check_vma=False,
    )
```

```python
import functools
import math

import jax
import jax.numpy as jnp
from jax import lax
from jax.experimental import pallas as pl
from jax.experimental.pallas import tpu as pltpu
from jax.sharding import PartitionSpec as P

MESH = pl.DeviceIdType.MESH
HEADS = 4
DEPTH = 128
SLOTS = 3
SPAN = 128
ROWS = SLOTS * SPAN
WIDTH = HEADS * DEPTH
MODEL = 1024
CHIPS = 16
RING = 32
EPSILON = 1e-06
SCALE = 1.0 / math.sqrt(DEPTH)
F32 = jnp.float32
BF16 = jnp.bfloat16


OTHER_CHIPS = sorted(
    ((i // 4, i % 4) for i in range(1, CHIPS)), key=lambda d: -(min(d[0], 4 - d[0]) + min(d[1], 4 - d[1]))
)
PLACES = (0, -1, 1, -2, 2, -3, 3, -4)


def dot(a, b, ca, cb):
    return lax.dot_general(a, b, (((ca,), (cb,)), ((), ())), preferred_element_type=F32)


def layer_kernel(
    total_seqs,
    events_hbm, weight_hbm, keys_hbm, values_hbm, gates_hbm, upstream_hbm, lengths_hbm,
    grad_keys_hbm, grad_values_hbm, grad_gates_hbm, grad_weight_ref,
    ev, kk, vv, gg, uu, lens,
    wf, wun, evt, gn, qq, att, dact, gm, gs, gq, out_k, out_v, out_g,
    gbuf, cbuf, sbuf, rbuf, tbuf, zbuf, gw,
    in_sem, near_s, near_r, rel_s, rel_r, ag_s, ag_r, cw_s, cw_r,
    cg_s, cg_r, rs_s, rs_r, zr_s, zr_r, fin_s, fin_r, out_sem,
):
    dp = lax.axis_index("dp")
    z = lax.axis_index("fsdp")
    core = lax.rem(dp, 2)
    chip = dp // 2
    x = chip // 4
    y = lax.rem(chip, 4)
    phase = lax.rem(y - z + RING, 4)
    is_source = lax.rem(z, 4) == y

    def ring_at(offset):
        return {"dp": dp, "fsdp": lax.rem(z + offset + RING, RING)}

    def chip_at(dx, dy, other_core):
        return {"dp": (lax.rem(x + dx, 4) * 4 + lax.rem(y + dy, 4)) * 2 + other_core, "fsdp": z}

    def remote(src, dst, ssem, rsem, device):
        return pltpu.make_async_remote_copy(
            src_ref=src, dst_ref=dst, send_sem=ssem, recv_sem=rsem,
            device_id=device, device_id_type=MESH,
        )

    partner = chip_at(0, 0, 1 - core)

    barrier = pltpu.get_barrier_semaphore()

    def tell(device):
        pl.semaphore_signal(barrier, inc=1, device_id=device, device_id_type=MESH)

    tell(ring_at(8))
    tell(ring_at(-8))
    for j in (-2, 1, -1):
        tell(ring_at(phase + 4 * j))

    @pl.when(phase != 0)
    def _():
        tell(ring_at(phase))

    for dx, dy in OTHER_CHIPS:
        tell(chip_at(dx, dy, core))
    tell(partner)
    loads = [
        pltpu.make_async_copy(src, dst, in_sem.at[i])
        for i, (src, dst) in enumerate(
            (
                (lengths_hbm, lens), (gates_hbm, gg), (upstream_hbm, uu),
                (events_hbm, ev), (keys_hbm, kk), (values_hbm, vv),
            )
        )
    ]
    for load in loads:
        load.start()

    pl.semaphore_wait(barrier, jnp.where(is_source, 33, 18))

    tile = weight_hbm.at[pl.ds(pl.multiple_of(core * 16, 16), 16), pl.ds(pl.multiple_of(x * 128, 128), 128)]
    own_tile = pltpu.make_async_copy(tile, wf.at[0, 0, core, x], near_r.at[0])
    near_sends = []
    for e in (8, -7, 7, -6, 6, -5, 5, -4, 4, -3, 3, -2, 2, -1, 1):
        ring_class = -e % 4
        place = PLACES.index((-e - ring_class) // 4)
        near_sends.append(
            remote(tile, wf.at[place, ring_class, core, x], near_s.at[e + 7], near_r.at[place], ring_at(e))
        )

    @pl.when(is_source)
    def _():
        for send in near_sends:
            send.start()
        own_tile.start()

    row_ids = lax.broadcasted_iota(jnp.int32, (SPAN, DEPTH), 0)
    col_ids = lax.broadcasted_iota(jnp.int32, (SPAN, DEPTH), 1)
    loads[0].wait()
    loads[1].wait()
    loads[2].wait()
    first_seq = (dp * RING + z) * SLOTS
    own_lens = [lens[first_seq + b] for b in range(SLOTS)]
    for b in range(SLOTS):
        rows = pl.ds(b * SPAN, SPAN)
        valid = row_ids < own_lens[b]
        parts = []
        for h in range(HEADS):
            cols = pl.ds(h * DEPTH, DEPTH)
            product = uu[rows, cols].astype(F32) * gg[rows, cols].astype(F32)
            parts.append(jnp.where(valid, product, 0.0))
        mean = jnp.sum(parts[0] + parts[1] + parts[2] + parts[3], axis=1, keepdims=True) * (1.0 / WIDTH)
        for h in range(HEADS):
            gn[rows, pl.ds(h * DEPTH, DEPTH)] = parts[h] - mean

    relays = []

    def relay(place):
        here = wf.at[place, phase, core, x]
        remote(here, here, near_s.at[0], near_r.at[place], partner).wait_recv()
        copy = remote(
            here, wf.at[place + 4, phase, core, x], rel_s.at[place], rel_r.at[place], ring_at(8 if place % 2 else -8)
        )
        copy.start()
        relays.append(copy)

    spreads = []

    def spread(group):
        piece = wf.at[pl.ds(2 * group, 2), phase, core, x]
        for dx, dy in OTHER_CHIPS:
            i = group * CHIPS + dx * 4 + dy
            send = remote(piece, piece, ag_s.at[i], ag_r.at[i], chip_at(dx, dy, core))
            send.start()
            spreads.append(send)

    swaps = []

    def swap(group):
        for dx, dy in reversed(OTHER_CHIPS):
            i = group * CHIPS + dx * 4 + dy
            other_class = lax.rem(lax.rem(y + 4 - dy, 4) - z + RING, 4)
            there = wf.at[pl.ds(2 * group, 2), other_class, core, lax.rem(x + 4 - dx, 4)]
            remote(there, there, ag_s.at[i], ag_r.at[i], partner).wait_recv()
        mine = wf.at[pl.ds(2 * group, 2), :, core]
        copy = remote(mine, mine, cw_s.at[group], cw_r.at[group], partner)
        copy.start()
        swaps.append(copy)

    def unpack(group):
        swaps[group].wait_recv()
        for place in (2 * group, 2 * group + 1):
            for ring_class in range(4):
                shard = lax.rem(z + ring_class + 4 * PLACES[place] + RING, RING)
                for half in range(2):
                    for c in range(4):
                        wun[shard, half, :, pl.ds(c * 128, 128)] = wf[place, ring_class, half, c]

    relay(0)
    relay(1)
    spread(0)
    relay(2)
    relay(3)
    spread(1)
    loads[3].wait()
    for m in range(0, MODEL, 128):
        evt[pl.ds(m, 128), :] = ev[:, pl.ds(m, 128)].T
    relays[0].wait_recv()
    relays[1].wait_recv()
    spread(2)
    swap(0)
    swap(1)
    relays[2].wait_recv()
    relays[3].wait_recv()
    spread(3)
    unpack(0)
    swap(2)
    unpack(1)
    loads[4].wait()
    loads[5].wait()
    swap(3)
    unpack(2)
    unpack(3)

    qq[...] = dot(ev[...], wun[...].reshape(MODEL, WIDTH), 1, 0).astype(BF16)
    for b in range(SLOTS):
        rows = pl.ds(b * SPAN, SPAN)
        inverse = 1.0 / jnp.full((1, DEPTH), own_lens[b].astype(F32))
        weight = jnp.where((col_ids <= row_ids) & (row_ids < own_lens[b]), inverse, 0.0)
        mixed = []
        for h in range(HEADS):
            cols = pl.ds(h * DEPTH, DEPTH)
            scores = dot(qq[rows, cols], kk[rows, cols], 1, 1) * SCALE
            sigmoid = 0.5 * jnp.tanh(0.5 * scores) + 0.5
            weighted = sigmoid * weight
            attention = (scores * weighted).astype(BF16)
            att[b * HEADS + h] = attention
            dact[b * HEADS + h] = weighted * (1.0 + scores * (1.0 - sigmoid))
            mixed.append(dot(attention, vv[rows, cols], 1, 0))
        mean = jnp.sum(mixed[0] + mixed[1] + mixed[2] + mixed[3], axis=1, keepdims=True) * (1.0 / WIDTH)
        centred = [m - mean for m in mixed]
        squares = [m * m for m in centred]
        var = jnp.sum(squares[0] + squares[1] + squares[2] + squares[3], axis=1, keepdims=True) * (1.0 / WIDTH)
        inv_std = lax.rsqrt(var + EPSILON)
        normed = [m * inv_std for m in centred]
        grads = [gn[rows, pl.ds(h * DEPTH, DEPTH)] for h in range(HEADS)]
        overlap = [g * n for g, n in zip(grads, normed)]
        slope = jnp.sum(overlap[0] + overlap[1] + overlap[2] + overlap[3], axis=1, keepdims=True) * (1.0 / WIDTH)
        for h in range(HEADS):
            cols = pl.ds(h * DEPTH, DEPTH)
            gm[rows, cols] = (inv_std * (grads[h] - normed[h] * slope)).astype(BF16)
            out_g[rows, cols] = (uu[rows, cols].astype(F32) * normed[h]).astype(BF16)

    core_sends = []
    rs_sends = []

    def reduce_head(h):
        core_sends[h].wait_recv()
        summed = gbuf[h, :, :, core].astype(F32) + cbuf[h].astype(F32)
        sbuf[h] = summed.astype(BF16)
        for dx, dy in OTHER_CHIPS:
            there_x, there_y = lax.rem(x + dx, 4), lax.rem(y + dy, 4)
            i = h * CHIPS + dx * 4 + dy
            send = remote(
                sbuf.at[h, pl.ds(2 * lax.rem(there_x + h, 4), 2), there_y], rbuf.at[chip, h],
                rs_s.at[i], rs_r.at[i], chip_at(dx, dy, core),
            )
            send.start()
            rs_sends.append(send)

    for h in range(HEADS):
        cols = pl.ds(h * DEPTH, DEPTH)
        for b in range(SLOTS):
            rows = pl.ds(b * SPAN, SPAN)
            grad_attention = dot(gm[rows, cols], vv[rows, cols], 1, 1)
            grad_scores = (grad_attention * dact[b * HEADS + h]).astype(BF16)
            gs[b * HEADS + h] = grad_scores
            gq[rows, :] = (dot(grad_scores, kk[rows, cols], 1, 0) * SCALE).astype(BF16)
        gbuf[h] = dot(evt[...], gq[...], 1, 0).astype(BF16).reshape(8, 4, 2, 16, 128)
        send = remote(gbuf.at[h, :, :, 1 - core], cbuf.at[h], cg_s.at[h], cg_r.at[h], partner)
        send.start()
        core_sends.append(send)
        if h > 0:
            reduce_head(h - 1)
    reduce_head(HEADS - 1)

    ring_sends = []
    for h in range(HEADS):
        pair = lax.rem(x + h, 4)
        total = sbuf[h, pl.ds(2 * pair, 2), y].astype(F32)
        for dx, dy in reversed(OTHER_CHIPS):
            i = h * CHIPS + dx * 4 + dy
            other = lax.rem(x + 4 - dx, 4) * 4 + lax.rem(y + 4 - dy, 4)
            there = rbuf.at[other, h]
            remote(there, there, rs_s.at[i], rs_r.at[i], partner).wait_recv()
            total = total + rbuf[other, h].astype(F32)
        tbuf[h] = total.astype(BF16)
        for k in range(2):
            target = 8 * pair + 4 * k + y
            send = remote(tbuf.at[h, k], zbuf.at[z], zr_s.at[2 * h + k], zr_r.at[z], {"dp": dp, "fsdp": target})
            ring_sends.append((target, send))

            @pl.when(target != z)
            def _():
                send.start()

    for b in range(SLOTS):
        rows = pl.ds(b * SPAN, SPAN)
        for h in range(HEADS):
            cols = pl.ds(h * DEPTH, DEPTH)
            out_v[rows, cols] = dot(att[b * HEADS + h], gm[rows, cols], 0, 0).astype(BF16)
            out_k[rows, cols] = (dot(gs[b * HEADS + h], qq[rows, cols], 0, 0) * SCALE).astype(BF16)
    stores = [
        pltpu.make_async_copy(src, dst, out_sem.at[i])
        for i, (src, dst) in enumerate(((out_k, grad_keys_hbm), (out_v, grad_values_hbm), (out_g, grad_gates_hbm)))
    ]
    for store in stores:
        store.start()

    head = lax.rem(z // 8 + 4 - x, 4)
    final_sends = []
    for dx, dy, swapped in [(dx, dy, k) for dx, dy in OTHER_CHIPS for k in range(2)] + [(0, 0, 1)]:
        there = gw.at[core, head]
        other_core = 1 - core if swapped else core
        final_sends.append(
            remote(
                there, there, fin_s.at[dx * 8 + dy * 2 + swapped], fin_r.at[x * 2 + core],
                chip_at(dx, dy, other_core),
            )
        )

    @pl.when(is_source)
    def _():
        acc = tbuf[head, lax.rem(z // 4, 2)].astype(F32)
        for i in range(1, RING):
            other = lax.rem(z + i, RING)
            there = zbuf.at[other]
            remote(there, there, zr_s.at[0], zr_r.at[other], partner).wait_recv()
            acc = acc + zbuf[other].astype(F32)
        gw[core, head] = (acc * (1.0 / total_seqs)).astype(BF16)
        for send in final_sends:
            send.start()

    source_y = lax.rem(z, 4)
    for sx in range(4):
        for sc in range(2):
            @pl.when((chip != sx * 4 + source_y) | (core != sc))
            def _():
                there = gw.at[sc, lax.rem(z // 8 + 4 - sx, 4)]
                remote(there, there, fin_s.at[0], fin_r.at[sx * 2 + sc], partner).wait_recv()
    for half in range(2):
        for h in range(HEADS):
            grad_weight_ref[pl.ds(half * 16, 16), pl.ds(h * DEPTH, DEPTH)] = gw[half, h].astype(F32)

    @pl.when(is_source)
    def _():
        for send in near_sends:
            send.wait_send()
        for send in final_sends:
            send.wait_send()

    for send in relays + spreads + swaps + core_sends + rs_sends:
        send.wait_send()
    for target, send in ring_sends:
        @pl.when(target != z)
        def _():
            send.wait_send()
    for store in stores:
        store.wait()


def store_kernel(*refs):
    count = (len(refs) - 2) // 3
    sources, results, held = refs[:count], refs[count : 2 * count], refs[2 * count : 3 * count]
    in_sem, out_sem = refs[-2:]
    loads = [pltpu.make_async_copy(a, b, in_sem.at[i]) for i, (a, b) in enumerate(zip(sources, held))]
    stores = [pltpu.make_async_copy(a, b, out_sem.at[i]) for i, (a, b) in enumerate(zip(held, results))]
    for load in loads:
        load.start()
    for load, store in zip(loads, stores):
        load.wait()
        store.start()
    for store in stores:
        store.wait()


def shards(events, query_weight, keys, values, gates, cotangent, lengths):
    flat = [a.reshape(ROWS, a.shape[2]) for a in (events, keys, values, gates, cotangent)]
    hbm = pl.BlockSpec(memory_space=pl.ANY)
    vmem = pltpu.VMEM
    dma = pltpu.SemaphoreType.DMA
    row_out = jax.ShapeDtypeStruct((ROWS, WIDTH), BF16)
    scratch = [
        vmem((ROWS, MODEL), BF16), vmem((ROWS, WIDTH), BF16), vmem((ROWS, WIDTH), BF16),
        vmem((ROWS, WIDTH), BF16), vmem((ROWS, WIDTH), BF16), pltpu.SMEM(lengths.shape, jnp.int32),
        vmem((8, 4, 2, 4, 16, 128), BF16), vmem((RING, 2, 16, WIDTH), BF16), vmem((MODEL, ROWS), BF16),
        vmem((ROWS, WIDTH), F32), vmem((ROWS, WIDTH), BF16), vmem((12, SPAN, SPAN), BF16),
        vmem((12, SPAN, SPAN), F32), vmem((ROWS, WIDTH), BF16), vmem((12, SPAN, SPAN), BF16),
        vmem((ROWS, DEPTH), BF16),
        vmem((ROWS, WIDTH), BF16), vmem((ROWS, WIDTH), BF16), vmem((ROWS, WIDTH), BF16),
        vmem((4, 8, 4, 2, 16, 128), BF16), vmem((4, 8, 4, 16, 128), BF16), vmem((4, 8, 4, 16, 128), BF16),
        vmem((16, 4, 2, 16, 128), BF16), vmem((4, 2, 16, 128), BF16), vmem((RING, 16, 128), BF16),
        vmem((2, 4, 16, 128), BF16),
        dma((6,)), dma((16,)), dma((4,)), dma((4,)), dma((4,)), dma((64,)), dma((64,)),
        dma((4,)), dma((4,)), dma((4,)), dma((4,)), dma((64,)), dma((64,)), dma((8,)), dma((32,)),
        dma((32,)), dma((8,)), dma((3,)),
    ]
    grad_keys, grad_values, grad_gates, grad_weight = pl.pallas_call(
        functools.partial(layer_kernel, lengths.shape[0]),
        out_shape=(row_out, row_out, row_out, jax.ShapeDtypeStruct((32, WIDTH), F32)),
        in_specs=[hbm] * 7,
        out_specs=(hbm, hbm, hbm, pl.BlockSpec(memory_space=vmem)),
        scratch_shapes=scratch,
        compiler_params=pltpu.CompilerParams(
            collective_id=0, has_side_effects=True, vmem_limit_bytes=60 * 2**20
        ),
        name="layer",
    )(flat[0], query_weight, flat[1], flat[2], flat[3], flat[4], lengths)
    results = (grad_keys, grad_values, grad_gates, grad_weight)
    grad_keys, grad_values, grad_gates, grad_weight = pl.pallas_call(
        store_kernel,
        out_shape=tuple(jax.ShapeDtypeStruct(r.shape, r.dtype) for r in results),
        in_specs=[hbm] * 4,
        out_specs=(hbm,) * 4,
        scratch_shapes=[vmem(r.shape, r.dtype) for r in results] + [dma((4,)), dma((4,))],
        compiler_params=pltpu.CompilerParams(vmem_limit_bytes=60 * 2**20),
        name="store",
    )(*results)
    shape = keys.shape
    return grad_keys.reshape(shape), grad_values.reshape(shape), grad_gates.reshape(shape), grad_weight


def solution(mesh):
    by_seq = P(("dp", "fsdp"), None, None)
    return jax.shard_map(
        shards,
        mesh=mesh,
        in_specs=(by_seq, P("fsdp", None), by_seq, by_seq, by_seq, by_seq, P()),
        out_specs=(by_seq, by_seq, by_seq, P("fsdp", None)),
        check_vma=False,
    )
```

```python
import functools
import math

import jax
import jax.numpy as jnp
from jax import lax
from jax.experimental import pallas as pl
from jax.experimental.pallas import tpu as pltpu
from jax.sharding import PartitionSpec as P

MESH = pl.DeviceIdType.MESH
HEADS = 4
DEPTH = 128
SLOTS = 3
SPAN = 128
ROWS = SLOTS * SPAN
WIDTH = HEADS * DEPTH
MODEL = 1024
CHIPS = 16
RING = 32
EPSILON = 1e-06
SCALE = 1.0 / math.sqrt(DEPTH)
F32 = jnp.float32
BF16 = jnp.bfloat16


OTHER_CHIPS = sorted(
    ((i // 4, i % 4) for i in range(1, CHIPS)), key=lambda d: -(min(d[0], 4 - d[0]) + min(d[1], 4 - d[1]))
)
PLACES = (0, -1, 1, -2, 2, -3, 3, -4)


def dot(a, b, ca, cb):
    return lax.dot_general(a, b, (((ca,), (cb,)), ((), ())), preferred_element_type=F32)


def layer_kernel(
    total_seqs,
    events_hbm, weight_hbm, keys_hbm, values_hbm, gates_hbm, upstream_hbm, lengths_hbm,
    grad_keys_hbm, grad_values_hbm, grad_gates_hbm, gw_hbm,
    ev, kk, vv, gg, uu, lens,
    wf, wun, evt, gn, qq, att, dact, gm, gs, gq, out_k, out_v, out_g,
    gbuf, cbuf, sbuf, rbuf, tbuf, zbuf, gw,
    in_sem, near_s, near_r, rel_s, rel_r, ag_s, ag_r, cw_s, cw_r,
    cg_s, cg_r, rs_s, rs_r, zr_s, zr_r, fin_s, fin_r, out_sem,
):
    dp = lax.axis_index("dp")
    z = lax.axis_index("fsdp")
    core = lax.rem(dp, 2)
    chip = dp // 2
    x = chip // 4
    y = lax.rem(chip, 4)
    phase = lax.rem(y - z + RING, 4)
    is_source = lax.rem(z, 4) == y

    def ring_at(offset):
        return {"dp": dp, "fsdp": lax.rem(z + offset + RING, RING)}

    def chip_at(dx, dy, other_core):
        return {"dp": (lax.rem(x + dx, 4) * 4 + lax.rem(y + dy, 4)) * 2 + other_core, "fsdp": z}

    def remote(src, dst, ssem, rsem, device):
        return pltpu.make_async_remote_copy(
            src_ref=src, dst_ref=dst, send_sem=ssem, recv_sem=rsem,
            device_id=device, device_id_type=MESH,
        )

    partner = chip_at(0, 0, 1 - core)

    barrier = pltpu.get_barrier_semaphore()

    def tell(device):
        pl.semaphore_signal(barrier, inc=1, device_id=device, device_id_type=MESH)

    tell(ring_at(8))
    tell(ring_at(-8))
    for j in (-2, 1, -1):
        tell(ring_at(phase + 4 * j))

    @pl.when(phase != 0)
    def _():
        tell(ring_at(phase))

    for dx, dy in OTHER_CHIPS:
        tell(chip_at(dx, dy, core))
    tell(partner)
    loads = [
        pltpu.make_async_copy(src, dst, in_sem.at[i])
        for i, (src, dst) in enumerate(
            (
                (lengths_hbm, lens), (gates_hbm, gg), (upstream_hbm, uu),
                (events_hbm, ev), (keys_hbm, kk), (values_hbm, vv),
            )
        )
    ]
    for load in loads:
        load.start()

    pl.semaphore_wait(barrier, jnp.where(is_source, 33, 18))

    tile = weight_hbm.at[pl.ds(pl.multiple_of(core * 16, 16), 16), pl.ds(pl.multiple_of(x * 128, 128), 128)]
    own_tile = pltpu.make_async_copy(tile, wf.at[0, 0, core, x], near_r.at[0])
    near_sends = []
    for e in (8, -7, 7, -6, 6, -5, 5, -4, 4, -3, 3, -2, 2, -1, 1):
        ring_class = -e % 4
        place = PLACES.index((-e - ring_class) // 4)
        near_sends.append(
            remote(tile, wf.at[place, ring_class, core, x], near_s.at[e + 7], near_r.at[place], ring_at(e))
        )

    @pl.when(is_source)
    def _():
        for send in near_sends:
            send.start()
        own_tile.start()

    row_ids = lax.broadcasted_iota(jnp.int32, (SPAN, DEPTH), 0)
    col_ids = lax.broadcasted_iota(jnp.int32, (SPAN, DEPTH), 1)
    loads[0].wait()
    loads[1].wait()
    loads[2].wait()
    first_seq = (dp * RING + z) * SLOTS
    own_lens = [lens[first_seq + b] for b in range(SLOTS)]
    for b in range(SLOTS):
        rows = pl.ds(b * SPAN, SPAN)
        valid = row_ids < own_lens[b]
        parts = []
        for h in range(HEADS):
            cols = pl.ds(h * DEPTH, DEPTH)
            product = uu[rows, cols].astype(F32) * gg[rows, cols].astype(F32)
            parts.append(jnp.where(valid, product, 0.0))
        mean = jnp.sum(parts[0] + parts[1] + parts[2] + parts[3], axis=1, keepdims=True) * (1.0 / WIDTH)
        for h in range(HEADS):
            gn[rows, pl.ds(h * DEPTH, DEPTH)] = parts[h] - mean

    relays = []

    def relay(place):
        here = wf.at[place, phase, core, x]
        remote(here, here, near_s.at[0], near_r.at[place], partner).wait_recv()
        copy = remote(
            here, wf.at[place + 4, phase, core, x], rel_s.at[place], rel_r.at[place], ring_at(8 if place % 2 else -8)
        )
        copy.start()
        relays.append(copy)

    spreads = []

    def spread(group):
        piece = wf.at[pl.ds(2 * group, 2), phase, core, x]
        for dx, dy in OTHER_CHIPS:
            i = group * CHIPS + dx * 4 + dy
            send = remote(piece, piece, ag_s.at[i], ag_r.at[i], chip_at(dx, dy, core))
            send.start()
            spreads.append(send)

    swaps = []

    def swap(group):
        for dx, dy in reversed(OTHER_CHIPS):
            i = group * CHIPS + dx * 4 + dy
            other_class = lax.rem(lax.rem(y + 4 - dy, 4) - z + RING, 4)
            there = wf.at[pl.ds(2 * group, 2), other_class, core, lax.rem(x + 4 - dx, 4)]
            remote(there, there, ag_s.at[i], ag_r.at[i], partner).wait_recv()
        mine = wf.at[pl.ds(2 * group, 2), :, core]
        copy = remote(mine, mine, cw_s.at[group], cw_r.at[group], partner)
        copy.start()
        swaps.append(copy)

    def unpack(group):
        swaps[group].wait_recv()
        for place in (2 * group, 2 * group + 1):
            for ring_class in range(4):
                shard = lax.rem(z + ring_class + 4 * PLACES[place] + RING, RING)
                for half in range(2):
                    for c in range(4):
                        wun[shard, half, :, pl.ds(c * 128, 128)] = wf[place, ring_class, half, c]

    relay(0)
    relay(1)
    spread(0)
    relay(2)
    relay(3)
    spread(1)
    loads[3].wait()
    for m in range(0, MODEL, 128):
        evt[pl.ds(m, 128), :] = ev[:, pl.ds(m, 128)].T
    relays[0].wait_recv()
    relays[1].wait_recv()
    spread(2)
    swap(0)
    swap(1)
    relays[2].wait_recv()
    relays[3].wait_recv()
    spread(3)
    unpack(0)
    swap(2)
    unpack(1)
    loads[4].wait()
    loads[5].wait()
    swap(3)
    unpack(2)
    unpack(3)

    qq[...] = dot(ev[...], wun[...].reshape(MODEL, WIDTH), 1, 0).astype(BF16)
    for b in range(SLOTS):
        rows = pl.ds(b * SPAN, SPAN)
        inverse = 1.0 / jnp.full((1, DEPTH), own_lens[b].astype(F32))
        weight = jnp.where((col_ids <= row_ids) & (row_ids < own_lens[b]), inverse, 0.0)
        mixed = []
        for h in range(HEADS):
            cols = pl.ds(h * DEPTH, DEPTH)
            scores = dot(qq[rows, cols], kk[rows, cols], 1, 1) * SCALE
            sigmoid = 0.5 * jnp.tanh(0.5 * scores) + 0.5
            weighted = sigmoid * weight
            attention = (scores * weighted).astype(BF16)
            att[b * HEADS + h] = attention
            dact[b * HEADS + h] = weighted * (1.0 + scores * (1.0 - sigmoid))
            mixed.append(dot(attention, vv[rows, cols], 1, 0))
        mean = jnp.sum(mixed[0] + mixed[1] + mixed[2] + mixed[3], axis=1, keepdims=True) * (1.0 / WIDTH)
        centred = [m - mean for m in mixed]
        squares = [m * m for m in centred]
        var = jnp.sum(squares[0] + squares[1] + squares[2] + squares[3], axis=1, keepdims=True) * (1.0 / WIDTH)
        inv_std = lax.rsqrt(var + EPSILON)
        normed = [m * inv_std for m in centred]
        grads = [gn[rows, pl.ds(h * DEPTH, DEPTH)] for h in range(HEADS)]
        overlap = [g * n for g, n in zip(grads, normed)]
        slope = jnp.sum(overlap[0] + overlap[1] + overlap[2] + overlap[3], axis=1, keepdims=True) * (1.0 / WIDTH)
        for h in range(HEADS):
            cols = pl.ds(h * DEPTH, DEPTH)
            gm[rows, cols] = (inv_std * (grads[h] - normed[h] * slope)).astype(BF16)
            out_g[rows, cols] = (uu[rows, cols].astype(F32) * normed[h]).astype(BF16)

    core_sends = []
    rs_sends = []

    def reduce_head(h):
        core_sends[h].wait_recv()
        summed = gbuf[h, :, :, core].astype(F32) + cbuf[h].astype(F32)
        sbuf[h] = summed.astype(BF16)
        for dx, dy in OTHER_CHIPS:
            there_x, there_y = lax.rem(x + dx, 4), lax.rem(y + dy, 4)
            i = h * CHIPS + dx * 4 + dy
            send = remote(
                sbuf.at[h, pl.ds(2 * lax.rem(there_x + h, 4), 2), there_y], rbuf.at[chip, h],
                rs_s.at[i], rs_r.at[i], chip_at(dx, dy, core),
            )
            send.start()
            rs_sends.append(send)

    for h in range(HEADS):
        cols = pl.ds(h * DEPTH, DEPTH)
        for b in range(SLOTS):
            rows = pl.ds(b * SPAN, SPAN)
            grad_attention = dot(gm[rows, cols], vv[rows, cols], 1, 1)
            grad_scores = (grad_attention * dact[b * HEADS + h]).astype(BF16)
            gs[b * HEADS + h] = grad_scores
            gq[rows, :] = (dot(grad_scores, kk[rows, cols], 1, 0) * SCALE).astype(BF16)
        gbuf[h] = dot(evt[...], gq[...], 1, 0).astype(BF16).reshape(8, 4, 2, 16, 128)
        send = remote(gbuf.at[h, :, :, 1 - core], cbuf.at[h], cg_s.at[h], cg_r.at[h], partner)
        send.start()
        core_sends.append(send)
        if h > 0:
            reduce_head(h - 1)
    reduce_head(HEADS - 1)

    ring_sends = []
    for h in range(HEADS):
        pair = lax.rem(x + h, 4)
        total = sbuf[h, pl.ds(2 * pair, 2), y].astype(F32)
        for dx, dy in reversed(OTHER_CHIPS):
            i = h * CHIPS + dx * 4 + dy
            other = lax.rem(x + 4 - dx, 4) * 4 + lax.rem(y + 4 - dy, 4)
            there = rbuf.at[other, h]
            remote(there, there, rs_s.at[i], rs_r.at[i], partner).wait_recv()
            total = total + rbuf[other, h].astype(F32)
        tbuf[h] = total.astype(BF16)
        for k in range(2):
            target = 8 * pair + 4 * k + y
            send = remote(tbuf.at[h, k], zbuf.at[z], zr_s.at[2 * h + k], zr_r.at[z], {"dp": dp, "fsdp": target})
            ring_sends.append((target, send))

            @pl.when(target != z)
            def _():
                send.start()

    for b in range(SLOTS):
        rows = pl.ds(b * SPAN, SPAN)
        for h in range(HEADS):
            cols = pl.ds(h * DEPTH, DEPTH)
            out_v[rows, cols] = dot(att[b * HEADS + h], gm[rows, cols], 0, 0).astype(BF16)
            out_k[rows, cols] = (dot(gs[b * HEADS + h], qq[rows, cols], 0, 0) * SCALE).astype(BF16)
    stores = [
        pltpu.make_async_copy(src, dst, out_sem.at[i])
        for i, (src, dst) in enumerate(((out_k, grad_keys_hbm), (out_v, grad_values_hbm), (out_g, grad_gates_hbm)))
    ]
    for store in stores:
        store.start()

    @pl.when(is_source)
    def _():
        for send in near_sends:
            send.wait_send()

    for send in relays + spreads + swaps + core_sends + rs_sends:
        send.wait_send()
    for store in stores:
        store.wait()

    head = lax.rem(z // 8 + 4 - x, 4)
    own_result = pltpu.make_async_copy(gw, gw_hbm.at[core, head], fin_s.at[0])
    final_sends = []
    for dx, dy, swapped in [(dx, dy, k) for dx, dy in OTHER_CHIPS for k in range(2)] + [(0, 0, 1)]:
        other_core = 1 - core if swapped else core
        final_sends.append(
            remote(
                gw, gw_hbm.at[core, head], fin_s.at[dx * 8 + dy * 2 + swapped], fin_r.at[x * 2 + core],
                chip_at(dx, dy, other_core),
            )
        )

    @pl.when(is_source)
    def _():
        acc = tbuf[head, lax.rem(z // 4, 2)].astype(F32)
        for i in range(1, RING):
            other = lax.rem(z + i, RING)
            there = zbuf.at[other]
            remote(there, there, zr_s.at[0], zr_r.at[other], partner).wait_recv()
            acc = acc + zbuf[other].astype(F32)
        gw[...] = (acc * (1.0 / total_seqs)).astype(BF16)
        for send in final_sends:
            send.start()
        own_result.start()

    source_y = lax.rem(z, 4)
    for sx in range(4):
        for sc in range(2):
            @pl.when((chip != sx * 4 + source_y) | (core != sc))
            def _():
                there = gw_hbm.at[sc, lax.rem(z // 8 + 4 - sx, 4)]
                remote(there, there, fin_s.at[1], fin_r.at[sx * 2 + sc], partner).wait_recv()
    @pl.when(is_source)
    def _():
        for send in final_sends:
            send.wait_send()
        own_result.wait()

    for target, send in ring_sends:
        @pl.when(target != z)
        def _():
            send.wait_send()


def store_kernel(*refs):
    sources, results, held = refs[:4], refs[4:8], refs[8:12]
    wide, in_sem, out_sem = refs[12:]
    loads = [pltpu.make_async_copy(a, b, in_sem.at[i]) for i, (a, b) in enumerate(zip(sources, held))]
    stores = [
        pltpu.make_async_copy(a, b, out_sem.at[i]) for i, (a, b) in enumerate(zip((*held[:3], wide), results))
    ]
    for load in loads:
        load.start()
    for load, store in zip(loads[:3], stores[:3]):
        load.wait()
        store.start()
    loads[3].wait()
    for half in range(2):
        for h in range(HEADS):
            wide[pl.ds(half * 16, 16), pl.ds(h * DEPTH, DEPTH)] = held[3][half, h].astype(F32)
    stores[3].start()
    for store in stores:
        store.wait()


def shards(events, query_weight, keys, values, gates, cotangent, lengths):
    flat = [a.reshape(ROWS, a.shape[2]) for a in (events, keys, values, gates, cotangent)]
    hbm = pl.BlockSpec(memory_space=pl.ANY)
    vmem = pltpu.VMEM
    dma = pltpu.SemaphoreType.DMA
    row_out = jax.ShapeDtypeStruct((ROWS, WIDTH), BF16)
    scratch = [
        vmem((ROWS, MODEL), BF16), vmem((ROWS, WIDTH), BF16), vmem((ROWS, WIDTH), BF16),
        vmem((ROWS, WIDTH), BF16), vmem((ROWS, WIDTH), BF16), pltpu.SMEM(lengths.shape, jnp.int32),
        vmem((8, 4, 2, 4, 16, 128), BF16), vmem((RING, 2, 16, WIDTH), BF16), vmem((MODEL, ROWS), BF16),
        vmem((ROWS, WIDTH), F32), vmem((ROWS, WIDTH), BF16), vmem((12, SPAN, SPAN), BF16),
        vmem((12, SPAN, SPAN), F32), vmem((ROWS, WIDTH), BF16), vmem((12, SPAN, SPAN), BF16),
        vmem((ROWS, DEPTH), BF16),
        vmem((ROWS, WIDTH), BF16), vmem((ROWS, WIDTH), BF16), vmem((ROWS, WIDTH), BF16),
        vmem((4, 8, 4, 2, 16, 128), BF16), vmem((4, 8, 4, 16, 128), BF16), vmem((4, 8, 4, 16, 128), BF16),
        vmem((16, 4, 2, 16, 128), BF16), vmem((4, 2, 16, 128), BF16), vmem((RING, 16, 128), BF16),
        vmem((16, 128), BF16),
        dma((6,)), dma((16,)), dma((4,)), dma((4,)), dma((4,)), dma((64,)), dma((64,)),
        dma((4,)), dma((4,)), dma((4,)), dma((4,)), dma((64,)), dma((64,)), dma((8,)), dma((32,)),
        dma((32,)), dma((8,)), dma((3,)),
    ]
    grad_keys, grad_values, grad_gates, grad_weight = pl.pallas_call(
        functools.partial(layer_kernel, lengths.shape[0]),
        out_shape=(row_out, row_out, row_out, jax.ShapeDtypeStruct((2, HEADS, 16, DEPTH), BF16)),
        in_specs=[hbm] * 7,
        out_specs=(hbm,) * 4,
        scratch_shapes=scratch,
        compiler_params=pltpu.CompilerParams(
            collective_id=0, has_side_effects=True, vmem_limit_bytes=60 * 2**20
        ),
        name="layer",
    )(flat[0], query_weight, flat[1], flat[2], flat[3], flat[4], lengths)
    results = (grad_keys, grad_values, grad_gates, grad_weight)
    grad_keys, grad_values, grad_gates, grad_weight = pl.pallas_call(
        store_kernel,
        out_shape=(row_out, row_out, row_out, jax.ShapeDtypeStruct((32, WIDTH), F32)),
        in_specs=[hbm] * 4,
        out_specs=(hbm,) * 4,
        scratch_shapes=[vmem(r.shape, r.dtype) for r in results] + [vmem((32, WIDTH), F32), dma((4,)), dma((4,))],
        compiler_params=pltpu.CompilerParams(vmem_limit_bytes=60 * 2**20),
        name="store",
    )(*results)
    shape = keys.shape
    return grad_keys.reshape(shape), grad_values.reshape(shape), grad_gates.reshape(shape), grad_weight


def solution(mesh):
    by_seq = P(("dp", "fsdp"), None, None)
    return jax.shard_map(
        shards,
        mesh=mesh,
        in_specs=(by_seq, P("fsdp", None), by_seq, by_seq, by_seq, by_seq, P()),
        out_specs=(by_seq, by_seq, by_seq, P("fsdp", None)),
        check_vma=False,
    )
```
